256 devices in a mesh: seq: 64 (over z, y, core), head: 4 (over x).
Axes of the slice: x: 4, y: 4, z: 8, core: 2. Of those that a mesh axis runs over, the one named last changes fastest.
Arguments:
- queries: bfloat16 [32768, 2048], P('seq', 'head'), may hold values from -8.4 to 8.4, as said below
- keyval: bfloat16 [2, 32768, 512], P(None, 'seq', 'head'), may hold values from -16 to 16, as said below
- gates: int32 [64, 8], replicated, may hold values from -1 to 63, as said below
- pair_block: int32 [32], replicated, may hold values from 0 to 31, each once
- out_weight: bfloat16 [2048, 4096], P('head'), may hold values from -0.125 to 0.125
Outputs:
- layer_out: bfloat16 [32768, 4096], P(('seq', 'head'))
The draws below stay inside these ranges and needn't reach their ends.
Inputs may be any that keep to these rules, and one draw needn't show every extreme that they name: Values of queries lie within the bounds. Values of keyval lie within the bounds. `gates`: row b names distinct blocks at or before b; its first entry is b itself; unused entries are -1 and follow the used ones. For every b < 32 and every k < 32 with k != b, the rows b and 63 - b together name at most one of the blocks k and 63 - k.
All inputs are finite; a program needn't handle non-finite values.
Results may differ from the reference program's by a relative error of at most 0.0053.
Values may be sent and summed in bfloat16 or wider, within the bound.
A program may use at most 128 MiB of HBM per device.

```python
import jax
import jax.numpy as jnp
from jax import lax

D = 4096
HEADS = 16
KVH = 4
HD = 128
BLOCK = 512
TOPK = 8
TOKENS = 32768
BLOCKS = 64
N_SEQ = 64


def draw_queries(key, part):
    key = jax.random.fold_in(key, 1)
    return jnp.clip(1.4 * jax.random.normal(key, (TOKENS, HEADS * HD)), -8.4, 8.4).astype(jnp.bfloat16)


def draw_keyval(key, part):
    key = jax.random.fold_in(key, 2)
    key_part = jnp.clip(1.4 * jax.random.normal(jax.random.fold_in(key, 4), (TOKENS, KVH * HD)), -8.4, 8.4)
    value_part = jnp.clip(4.0 * jax.random.normal(jax.random.fold_in(key, 5), (TOKENS, KVH * HD)), -16.0, 16.0)
    return jnp.stack([key_part, value_part]).astype(jnp.bfloat16)


def draw_gates(key, part):
    key = jax.random.fold_in(key, 3)
    row_index = jnp.arange(BLOCKS)[:, None]
    col_index = jnp.arange(BLOCKS)[None, :]
    row_pair = jnp.minimum(row_index, BLOCKS - 1 - row_index)
    col_pair = jnp.minimum(col_index, BLOCKS - 1 - col_index)
    side_bits = jax.random.randint(jax.random.fold_in(key, 1), (BLOCKS // 2, BLOCKS // 2), 0, 2)
    row_sides = jnp.take(side_bits, row_pair[:, 0], axis=0)
    chosen_side = jnp.take(row_sides, col_pair[0], axis=1)
    late_column = (col_index >= BLOCKS // 2).astype(jnp.int32)
    allowed = (chosen_side == late_column) | (col_pair == row_pair)
    candidate = allowed & (col_index < row_index)
    noise_score = jax.random.randint(jax.random.fold_in(key, 2), (BLOCKS, BLOCKS), 0, 1000)
    boost_score = jnp.where((col_index == 0) | (col_index == row_index - 1), 2000, 0)
    total_score = jnp.where(candidate, (noise_score + boost_score) * BLOCKS + col_index, -1)
    top_values, top_index = lax.top_k(total_score, TOPK - 1)
    chosen = jnp.where(top_values >= 0, top_index, -1)
    return jnp.concatenate([jnp.broadcast_to(row_index, (BLOCKS, 1)), chosen], axis=1).astype(jnp.int32)


def level_of(rng, extent, shards, low, top_value):
    factor_of, own = 1.0, jax.random.fold_in(rng, 6)
    for dim, shards_of in shards:
        heights = jnp.exp(jax.random.uniform(jax.random.fold_in(own, dim), (shards_of,), jnp.float32, low / len(shards), top_value / len(shards)))
        factor_of = factor_of * jnp.repeat(heights, extent[dim] // shards_of).reshape([-1 if axis == dim else 1 for axis in range(len(extent))])
    return factor_of


def scatter_about(stream_key, extent, scale, bound, pieces=(), kind=jnp.bfloat16):
    factor_of = level_of(stream_key, extent, pieces, -0.22, 0.18) if pieces else 1.0
    values = jax.random.normal(stream_key, extent, jnp.float32) * scale * factor_of
    return jnp.minimum(jnp.maximum(values, -bound), bound).astype(kind)


def setup_inputs(seed: int = 0) -> dict:
    seeds = jax.random.split(jax.random.key(seed), 6)
    return {
        "queries": draw_queries(jax.random.fold_in(seeds[5], 71), 0),
        "keyval": draw_keyval(jax.random.fold_in(seeds[5], 71), 0),
        "gates": draw_gates(jax.random.fold_in(seeds[5], 71), 0),
        "pair_block": jax.random.permutation(seeds[3], N_SEQ // 2).astype(jnp.int32),
        "out_weight": scatter_about(seeds[4], (HEADS * HD, D), (HEADS * HD) ** -0.5, 0.125, ((0, 4),)),
    }


def attend(query_rows, picked, entries, own_block, offset):
    key_span = picked.shape[1]
    half_rows = query_rows.shape[0]
    per_entry = key_span // entries.shape[0]
    scores = jnp.einsum('qkgd,lkd->kgql', query_rows.astype(jnp.float32), picked[0].astype(jnp.float32)) / jnp.sqrt(jnp.float32(HD))
    listed = jnp.broadcast_to(entries[:, None], (entries.shape[0], per_entry)).reshape(key_span)
    key_pos = jnp.arange(key_span, dtype=jnp.int32) % per_entry
    query_pos = offset + jnp.arange(half_rows, dtype=jnp.int32)
    allowed = (listed >= 0)[None, :] & ((listed != own_block)[None, :] | (key_pos[None, :] <= query_pos[:, None]))
    masked = jnp.where(allowed, scores, jnp.float32(-1e+30))
    row_peak = lax.optimization_barrier(jnp.max(masked, axis=-1, keepdims=True))
    weights = jnp.where(allowed, jnp.exp(masked - row_peak), jnp.float32(0.0))
    row_total = lax.optimization_barrier(jnp.sum(weights, axis=-1))
    rounded = weights.astype(jnp.bfloat16)
    blended = jnp.einsum('kgql,lkd->qkgd', rounded.astype(jnp.float32), picked[1].astype(jnp.float32))
    blended = blended / jnp.transpose(row_total, (2, 0, 1))[..., None]
    return blended.reshape(half_rows, -1).astype(jnp.bfloat16)

def reference(queries, keyval, gates, pair_block, out_weight):
    blocks = gates.shape[0]
    half_rows = BLOCK // 2
    group_size = HEADS // KVH
    kv_table = keyval.reshape(2, 2 * blocks, half_rows, KVH * HD)
    pair_range = jnp.arange(blocks // 2, dtype=jnp.int32)

    def one_piece(piece_id):
        device = piece_id // 2
        side_here = piece_id % 2
        pair_here = device // 2
        half_here = device % 2
        early_block = pair_block[pair_here]
        own_block = jnp.where(side_here == 0, early_block, blocks - 1 - early_block)
        entries = gates[own_block]
        match_early = entries[:, None] == pair_block[None, :]
        match_late = entries[:, None] == (blocks - 1 - pair_block)[None, :]
        owner_pair = lax.optimization_barrier(jnp.sum(jnp.where(match_early | match_late, pair_range[None, :], 0), axis=-1))
        slot_side = lax.optimization_barrier(jnp.sum(jnp.where(match_late, 1, 0), axis=-1))
        piece_index = ((2 * owner_pair[:, None] + jnp.arange(2, dtype=jnp.int32)[None, :]) * 2 + slot_side[:, None]).reshape(-1).astype(jnp.int32)
        picked = jnp.take(kv_table, piece_index, axis=1).reshape(2, TOPK * BLOCK, KVH, HD)
        query_rows = lax.dynamic_slice_in_dim(queries, (piece_id * half_rows).astype(jnp.int32), half_rows, 0)
        query_rows = query_rows.reshape(half_rows, KVH, group_size, HD)
        return attend(query_rows, picked, entries, own_block, half_here * half_rows)
    attended = lax.map(one_piece, jnp.arange(2 * blocks, dtype=jnp.int32)).reshape(queries.shape)
    return jnp.dot(attended, out_weight, preferred_element_type=jnp.float32).astype(jnp.bfloat16)
```

```python
import jax
import jax.numpy as jnp
from jax import lax
from jax.experimental import pallas as pl
from jax.experimental.pallas import tpu as pltpu
from jax.sharding import PartitionSpec as P

HD = 128
TOPK = 8
HALF = 256
R1 = 192
R2 = HALF - R1
NZ, NY, NX = 8, 4, 4
SCALE = 1.4426950408889634 / 128**0.5
NEG = -1e30
BIG = 1e30
WCH = ((0, 512), (512, 512), (1024, 512), (1536, 512))
ORDER = (2, 1, 3, 0)
f32, bf16 = jnp.float32, jnp.bfloat16


def mod(a, n):
    return lax.rem(a, jnp.int32(n))


def dot_nt(a, b):
    return lax.dot_general(a, b, (((1,), (1,)), ((), ())), preferred_element_type=f32)


def kernel(gates, pb, q, kvin, w, o, sel_k, sel_v, col_k, col_v, row_k, row_v, st1_k, st1_v, st2_k, st2_v,
           wbuf, s_acc, p_buf, l_buf, att_s, attg, bits, slots, valid,
           z1s, z1r, y2s, y2r, y1s, y1r, z2s, z2r, sbs, sbr, wss, wsr, wfs, wfr, wbs, wbr, ats, atr, wls):
    s = lax.axis_index("seq").astype(jnp.int32)
    x = lax.axis_index("head").astype(jnp.int32)
    z = lax.div(s, jnp.int32(8))
    y = mod(lax.div(s, jnp.int32(2)), 4)
    c = mod(s, 2)
    me = z * 4 + y
    sel, col, row = (sel_k, sel_v), (col_k, col_v), (row_k, row_v)
    st1, st2 = (st1_k, st1_v), (st2_k, st2_v)
    base = pl.multiple_of(c * HALF, HALF)

    def dev(zz, yy, cc, xx):
        return ((zz * 4 + yy) * 2 + cc, xx)

    def remote(src, dst, ssem, rsem, device):
        return pltpu.make_async_remote_copy(
            src_ref=src, dst_ref=dst, send_sem=ssem, recv_sem=rsem,
            device_id=device, device_id_type=pl.DeviceIdType.MESH)

    def z1(k, way, hop):
        step = 1 if way == 0 else NZ - 1
        zo = mod(z + (NZ - step) * (hop - 1), NZ)
        lo, n = (0, R1) if hop < 4 else ((0, R1 // 2) if way == 0 else (R1 // 2, R1 // 2))
        src = kvin.at[k, :, 0:R1] if hop == 1 else col[k].at[zo, :, lo:lo + n]
        return remote(src, col[k].at[zo, :, lo:lo + n], z1s.at[k, way, hop - 1], z1r.at[k, way, hop - 1],
                      dev(mod(z + step, NZ), y, c, x))

    def y2(k, d):
        return remote(kvin.at[k, :, R1:HALF], row[k].at[y], y2s.at[k, d - 1], y2r.at[k, d - 1],
                      dev(z, mod(y + d, NY), c, x))

    def y1(k, r, d):
        slot = mod(z + r, NZ) * 4 + y
        return remote(st1[k].at[r, d - 1], sel[k].at[slot, pl.ds(base, R1)], y1s.at[k, r, d - 1],
                      y1r.at[k, r, d - 1], dev(z, mod(y + d, NY), c, x))

    def z2(k, r, j):
        slot = z * 4 + mod(y + j, NY)
        return remote(st2[k].at[r, j], sel[k].at[slot, pl.ds(base + R1, R2)], z2s.at[k, r, j],
                      z2r.at[k, r, j], dev(mod(z + r, NZ), y, c, x))

    def sib(k, r):
        at = sel[k].at[pl.ds(mod(z + r, NZ) * 4, 4), pl.ds(base, HALF)]
        return remote(at, at, sbs.at[k, r], sbr.at[k, r], dev(z, y, 1 - c, x))

    def sib_own(k):
        at = sel[k].at[32, pl.ds(base, HALF)]
        return remote(at, at, sbs.at[k, 8], sbr.at[k, 8], dev(z, y, 1 - c, x))

    def wcols(i):
        off, n = WCH[i]
        return pl.ds(pl.multiple_of(c * 2048 + off, 128), n)

    def w1(way, i):
        step = 1 if way == 0 else NX - 1
        return remote(w.at[:, wcols(i)], wbuf.at[x, :, wcols(i)], wss.at[way, i], wsr.at[way, i],
                      dev(z, y, c, mod(x + step, NX)))

    def w2(way, i):
        step = 1 if way == 0 else NX - 1
        at = wbuf.at[mod(x + NX - step, NX), way * 256:way * 256 + 256, wcols(i)]
        return remote(at, at, wfs.at[way, i], wfr.at[way, i], dev(z, y, c, mod(x + step, NX)))

    def wsib(d, i):
        at = wbuf.at[mod(x + d, NX), :, wcols(i)]
        return remote(at, at, wbs.at[d - 1, i], wbr.at[d - 1, i], dev(z, y, 1 - c, x))

    def send_att(d):
        return remote(att_s.at[d - 1], attg.at[x], ats.at[d - 1], atr.at[d - 1], dev(z, y, c, mod(x + d, NX)))

    bar = pltpu.get_barrier_semaphore()
    peers = [dev(mod(z + r, NZ), y, c, x) for r in range(1, NZ)]
    peers += [dev(z, mod(y + d, NY), c, x) for d in range(1, NY)]
    peers += [dev(z, y, c, mod(x + d, NX)) for d in range(1, NX)]
    peers += [dev(z, y, 1 - c, x)]
    for p in peers:
        pl.semaphore_signal(bar, inc=1, device_id=p, device_id_type=pl.DeviceIdType.MESH)
    pl.semaphore_wait(bar, len(peers))

    for way in range(2):
        z1(0, way, 1).start()
    for d in range(1, NY):
        y2(0, d).start()
    own_w = pltpu.make_async_copy(w, wbuf.at[x], wls)
    own_w.start()
    for i in range(len(WCH)):
        for way in range(2):
            w1(way, i).start()

    def need(dest, base_at, origins):
        b = pb[dest]
        g = [gates[b, e] for e in range(TOPK)] + [gates[63 - b, e] for e in range(TOPK)]
        for i, origin in enumerate(origins):
            late = 63 - pb[origin]
            hit = g[0] == late
            for v in g[1:]:
                hit = hit | (v == late)
            bits[base_at + i] = jnp.where(hit, 1, 0)

    def need1(d, _):
        need(z * 4 + mod(y + d, NY), d * 8, [mod(z + r, NZ) * 4 + y for r in range(NZ)])
        return 0

    def need2(r, _):
        need(mod(z + r, NZ) * 4 + y, 32 + r * 4, [z * 4 + mod(y + j, NY) for j in range(NY)])
        return 0

    lax.fori_loop(0, NY, need1, 0)

    def put1(k, r):
        z0 = mod(z + r, NZ)
        if r == 0:
            a, b = kvin[k, 0, 0:R1], kvin[k, 1, 0:R1]
        else:
            a, b = col[k][z0, 0], col[k][z0, 1]
        for d in range(1, NY):
            st1[k][r, d - 1] = jnp.where(bits[d * 8 + r] > 0, b, a)
            y1(k, r, d).start()
        if r != 0:
            sel[k][z0 * 4 + y, pl.ds(base, R1)] = jnp.where(bits[r] > 0, b, a)

    def put2(k, j):
        yo = mod(y + j, NY)

        def one(r, _):
            if j == 0:
                a, b = kvin[k, 0, R1:HALF], kvin[k, 1, R1:HALF]
            else:
                a, b = row[k][yo, 0], row[k][yo, 1]
            st2[k][r, j] = jnp.where(bits[32 + r * 4 + j] > 0, b, a)
            z2(k, r, j).start()
            return 0

        lax.fori_loop(1, NZ, one, 0)
        if j != 0:
            a, b = row[k][yo, 0], row[k][yo, 1]
            sel[k][z * 4 + yo, pl.ds(base + R1, R2)] = jnp.where(bits[32 + j] > 0, b, a)

    def put_own(k):
        sel[k][me, pl.ds(base, HALF)] = kvin[k, 0]
        sel[k][32, pl.ds(base, HALF)] = kvin[k, 1]
        sib_own(k).start()

    def ring(k, hop):
        for way in range(2):
            z1(k, way, hop).wait_recv()
            if hop < 4:
                z1(k, way, hop + 1).start()
        for r in ((NZ - hop, hop) if hop < 4 else (4,)):
            put1(k, r)

    def rows_in(k):
        for d in range(1, NY):
            y2(k, d).wait_recv()
        for j in range(1, NY):
            put2(k, j)

    def collect(k, r):
        for d in range(1, NY):
            y1(k, r, d).wait_recv()
        if r != 0:
            for j in range(NY):
                z2(k, NZ - r, j).wait_recv()
        sib(k, r).start()

    put1(0, 0)
    lax.fori_loop(0, NZ, need2, 0)
    put_own(0)
    ring(0, 1)
    put2(0, 0)
    ring(0, 2)
    rows_in(0)
    ring(0, 3)
    ring(0, 4)

    own_early = pb[me]
    ent = [gates[own_early, e] for e in range(TOPK)] + [gates[63 - own_early, e] for e in range(TOPK)]

    def find(p, at):
        b = pb[p]
        return tuple(jnp.where((g == b) | (g == 63 - b), p, v) for g, v in zip(ent, at))

    at = lax.fori_loop(0, NZ * NY, find, tuple(jnp.int32(0) for _ in ent))
    for i, (g, v) in enumerate(zip(ent, at)):
        slots[i] = jnp.where(g == 63 - own_early, 32, jnp.where(g < 0, me, v))
        valid[i] = jnp.where(g >= 0, 1, 0)

    put_own(1)
    for way in range(2):
        z1(1, way, 1).start()
    for d in range(1, NY):
        y2(1, d).start()
    put1(1, 0)
    for r in (0, 1, 7, 2, 6, 3, 5, 4):
        collect(0, r)
    ring(1, 1)
    put2(1, 0)
    for r in range(NZ):
        sib(0, r).wait_recv()
    sib_own(0).wait_recv()

    def unit(u, _):
        di, hp = lax.div(u, jnp.int32(2)), mod(u, 2)
        d = jnp.where(di == 0, 2, jnp.where(di == 1, 1, jnp.where(di == 2, 3, 0)))
        dest = mod(x + d, NX)
        side8 = lax.div(dest, jnp.int32(2)) * 8
        qr = q[pl.ds(pl.multiple_of(dest * 128, 128), 128), pl.ds(pl.multiple_of(hp * 256, 256), 256)]
        qs = jnp.concatenate([qr[:, 0:128], qr[:, 128:256]], axis=0)
        hrow = pl.multiple_of(hp * 256, 256)
        qpos = mod(lax.broadcasted_iota(jnp.int32, (256, 128), 0), 128) + c * HALF + mod(dest, 2) * 128
        lane = lax.broadcasted_iota(jnp.int32, (256, 128), 1)
        m = jnp.full((256, 128), NEG, f32)
        for e in range(TOPK):
            sc = dot_nt(qs, sel_k[slots[side8 + e]])
            best = None
            for t in range(4):
                part = sc[:, t * 128:(t + 1) * 128]
                if e == 0:
                    part = jnp.where(lane + t * 128 <= qpos, part, NEG)
                s_acc[e, t] = part
                best = part if best is None else jnp.maximum(best, part)
            if e:
                best = jnp.where(valid[side8 + e] > 0, best, NEG)
            m = jnp.maximum(m, best)
        m = jnp.max(m, axis=1, keepdims=True)
        total = jnp.zeros((256, 128), f32)
        for e in range(TOPK):
            peak = m if e == 0 else jnp.where(valid[side8 + e] > 0, m, BIG)
            for t in range(4):
                p = jnp.exp2((s_acc[e, t] - peak) * SCALE)
                total = total + p
                p_buf[di, e, pl.ds(hrow, 256), t * 128:(t + 1) * 128] = p.astype(bf16)
        l_buf[di, pl.ds(hrow, 256)] = total
        return 0

    lax.fori_loop(0, 2, unit, 0)
    ring(1, 2)
    rows_in(1)
    lax.fori_loop(2, 4, unit, 0)
    ring(1, 3)
    ring(1, 4)
    lax.fori_loop(4, 8, unit, 0)
    for r in (0, 1, 7, 2, 6, 3, 5, 4):
        collect(1, r)
    for r in range(NZ):
        sib(1, r).wait_recv()
    sib_own(1).wait_recv()

    for i in range(len(WCH)):
        for way in range(2):
            w1(way, i).wait_recv()
            w2(way, i).start()
        wsib(1, i).start()
        wsib(3, i).start()

    for di, d in enumerate(ORDER):
        dest = mod(x + d, NX)
        side8 = lax.div(dest, jnp.int32(2)) * 8
        acc = jnp.zeros((512, 128), f32)
        for e in range(TOPK):
            acc = acc + jnp.dot(p_buf[di, e], sel_v[slots[side8 + e]], preferred_element_type=f32)
        out = (acc / jnp.sum(l_buf[di], axis=1, keepdims=True)).astype(bf16)
        for h in range(4):
            part = out[h * 128:(h + 1) * 128]
            if d == 0:
                attg[x, :, h * 128:(h + 1) * 128] = part
            else:
                att_s[d - 1, :, h * 128:(h + 1) * 128] = part
        if d:
            send_att(d).start()

    for i in range(len(WCH)):
        for way in range(2):
            w2(way, i).wait_recv()
        wsib(2, i).start()
    for i in range(len(WCH)):
        for d in range(1, NX):
            wsib(d, i).wait_recv()
    own_w.wait()
    for d in range(1, NX):
        send_att(d).wait_recv()

    def project(n, _):
        cols = pl.ds(pl.multiple_of(n * 512, 512), 512)
        acc = jnp.dot(attg[0], wbuf[0, :, cols], preferred_element_type=f32)
        for i in range(1, NX):
            acc = acc + jnp.dot(attg[i], wbuf[i, :, cols], preferred_element_type=f32)
        o[:, cols] = acc.astype(bf16)
        return 0

    lax.fori_loop(0, 8, project, 0)

    for k in range(2):
        for way in range(2):
            for hop in range(1, 5):
                z1(k, way, hop).wait_send()
        for d in range(1, NY):
            y2(k, d).wait_send()

        def done1(r, _, k=k):
            for d in range(1, NY):
                y1(k, r, d).wait_send()
            sib(k, r).wait_send()
            return 0

        def done2(r, _, k=k):
            for j in range(NY):
                z2(k, r, j).wait_send()
            return 0

        lax.fori_loop(0, NZ, done1, 0)
        lax.fori_loop(1, NZ, done2, 0)
        sib_own(k).wait_send()
    for i in range(len(WCH)):
        for way in range(2):
            w1(way, i).wait_send()
            w2(way, i).wait_send()
        for d in range(1, NX):
            wsib(d, i).wait_send()
    for d in range(1, NX):
        send_att(d).wait_send()


def body(queries, keyval, gates, pair_block, out_weight):
    kv = keyval.reshape(2, 2, HALF, HD)
    vmem, smem = pl.BlockSpec(memory_space=pltpu.VMEM), pl.BlockSpec(memory_space=pltpu.SMEM)
    n = len(WCH)
    dma = pltpu.SemaphoreType.DMA
    scratch = (
        [pltpu.VMEM((33, 512, HD), bf16)] * 2
        + [pltpu.VMEM((NZ, 2, R1, HD), bf16)] * 2
        + [pltpu.VMEM((NY, 2, R2, HD), bf16)] * 2
        + [pltpu.VMEM((NZ, 3, R1, HD), bf16)] * 2
        + [pltpu.VMEM((NZ, NY, R2, HD), bf16)] * 2
        + [
            pltpu.VMEM((NX, 512, 4096), bf16),
            pltpu.VMEM((TOPK, 4, 256, 128), f32),
            pltpu.VMEM((NX, TOPK, 512, 512), bf16),
            pltpu.VMEM((NX, 512, 128), f32),
            pltpu.VMEM((3, 128, 512), bf16),
            pltpu.VMEM((NX, 128, 512), bf16),
            pltpu.SMEM((64,), jnp.int32),
            pltpu.SMEM((16,), jnp.int32),
            pltpu.SMEM((16,), jnp.int32),
        ]
        + [dma((2, 2, 4))] * 2
        + [dma((2, 3))] * 2
        + [dma((2, NZ, 3))] * 2
        + [dma((2, NZ, NY))] * 2
        + [dma((2, 9))] * 2
        + [dma((2, n))] * 4
        + [dma((3, n))] * 2
        + [dma((3,))] * 2
        + [dma]
    )
    return pl.pallas_call(
        kernel,
        out_shape=jax.ShapeDtypeStruct((128, 4096), bf16),
        in_specs=[smem, smem, vmem, vmem, pl.BlockSpec(memory_space=pl.ANY)],
        out_specs=vmem,
        scratch_shapes=scratch,
        name="block_attention",
        cost_estimate=pl.CostEstimate(flops=6 * 2**30, bytes_accessed=8 * 2**20, transcendentals=8 * 2**20),
        compiler_params=pltpu.CompilerParams(
            collective_id=0, has_side_effects=True, vmem_limit_bytes=62 * 2**20),
    )(gates, pair_block, queries, kv, out_weight)


def solution(mesh):
    placed = (P("seq", "head"), P(None, "seq", "head"), P(), P(), P("head", None))
    return jax.shard_map(
        body, mesh=mesh, in_specs=placed, out_specs=P(("seq", "head"), None), check_vma=False
    )
```

```python
import jax
import jax.numpy as jnp
from jax import lax
from jax.experimental import pallas as pl
from jax.experimental.pallas import tpu as pltpu
from jax.sharding import PartitionSpec as P

HD = 128
TOPK = 8
HALF = 256
NZ, NY, NX = 8, 4, 4
SCALE = 1.4426950408889634 / 128**0.5
NEG = -1e30
BIG = 1e30
WS = ((0, 384), (384, 384))
WP = 768
WD = ((1536, 512),)
NS, NW = len(WS), len(WS) + len(WD)
ORDER = (2, 1, 3, 0)
STEPS = (
    ("R", 0, 0), ("W", 0), ("N1",), ("P", 0, 0), ("R", 1, 0), ("O", 0), ("O", 1), ("R", 0, 1), ("P", 0, 1),
    ("R", 1, 1), ("W", 1), ("R", 0, 2), ("P", 0, 2), ("R", 1, 2), ("R", 0, 3), ("P", 0, 3), ("X", 0), ("R", 1, 3),
    ("R", 0, 4), ("P", 0, 4), ("R", 1, 4), ("F",), ("C", 0, 0), ("C", 0, 1), ("C", 0, 7), ("X", 1), ("L", 0),
    ("W", 2), ("H", 0), ("D", 0, 2), ("D", 0, 6), ("P", 1, 0), ("C", 0, 2), ("C", 0, 6), ("D", 0, 3), ("D", 0, 5),
    ("P", 1, 1), ("C", 0, 3), ("C", 0, 5), ("D", 0, 4), ("P", 1, 2), ("C", 0, 4), ("S", 0), ("L", 1), ("H", 1),
    ("U", 0, 2), ("P", 1, 3), ("U", 2, 4), ("P", 1, 4), ("C", 1, 0), ("U", 4, 6), ("C", 1, 1), ("C", 1, 7),
    ("U", 6, 8), ("X", 2), ("C", 1, 2), ("C", 1, 6), ("C", 1, 3), ("C", 1, 5), ("C", 1, 4), ("G", 0), ("S", 1),
    ("V",), ("G", 1), ("L", 2), ("I",),
)
f32, bf16 = jnp.float32, jnp.bfloat16


def mod(a, n):
    return lax.rem(a, jnp.int32(n))


def dot_nt(a, b):
    return lax.dot_general(a, b, (((1,), (1,)), ((), ())), preferred_element_type=f32)


def kernel(gates, pb, q, kvin, w, o, sel_k, sel_v, col_k, col_v, st1_k, st1_v,
           wbuf, s_acc, p_buf, l_buf, att_s, attg, bits, slots, valid,
           z1s, z1r, y1s, y1r, sbs, sbr, wss, wsr, wfs, wfr, wbs, wbr, shs, shr, ats, atr, wls):
    s = lax.axis_index("seq").astype(jnp.int32)
    x = lax.axis_index("head").astype(jnp.int32)
    z = lax.div(s, jnp.int32(8))
    y = mod(lax.div(s, jnp.int32(2)), 4)
    c = mod(s, 2)
    me = z * 4 + y
    sel, col, st1 = (sel_k, sel_v), (col_k, col_v), (st1_k, st1_v)
    base = pl.multiple_of(c * HALF, HALF)

    def dev(zz, yy, cc, xx):
        return ((zz * 4 + yy) * 2 + cc, xx)

    def remote(src, dst, ssem, rsem, device):
        return pltpu.make_async_remote_copy(
            src_ref=src, dst_ref=dst, send_sem=ssem, recv_sem=rsem,
            device_id=device, device_id_type=pl.DeviceIdType.MESH)

    def z1(k, way, hop):
        step = 1 if way == 0 else NZ - 1
        zo = mod(z + (NZ - step) * (hop - 1), NZ)
        lo, n = (0, HALF) if hop < 4 else ((0, HALF // 2) if way == 0 else (HALF // 2, HALF // 2))
        src = kvin.at[k, :, 0:HALF] if hop == 1 else col[k].at[zo, :, lo:lo + n]
        return remote(src, col[k].at[zo, :, lo:lo + n], z1s.at[k, way, hop - 1], z1r.at[k, way, hop - 1],
                      dev(mod(z + step, NZ), y, c, x))

    def y1(k, r, d):
        slot = mod(z + r, NZ) * 4 + y
        return remote(st1[k].at[r, d - 1], sel[k].at[slot, pl.ds(base, HALF)], y1s.at[k, r, d - 1],
                      y1r.at[k, r, d - 1], dev(z, mod(y + d, NY), c, x))

    def sib(k, r):
        at = sel[k].at[pl.ds(mod(z + r, NZ) * 4, 4), pl.ds(base, HALF)]
        return remote(at, at, sbs.at[k, r], sbr.at[k, r], dev(z, y, 1 - c, x))

    def sib_own(k):
        at = sel[k].at[32, pl.ds(base, HALF)]
        return remote(at, at, sbs.at[k, 8], sbr.at[k, 8], dev(z, y, 1 - c, x))

    def wcols(i):
        if NS <= i < NW:
            off, n = WD[i - NS]
        else:
            off, n = WS[i % NW]
            off = off + mod(z + (0 if i < NS else 1), 2) * WP
        return pl.ds(pl.multiple_of(c * 2048 + off, 128), n)

    def w1(way, i):
        step = 1 if way == 0 else NX - 1
        return remote(w.at[:, wcols(i)], wbuf.at[x, :, wcols(i)], wss.at[way, i], wsr.at[way, i],
                      dev(z, y, c, mod(x + step, NX)))

    def w2(way, i):
        step = 1 if way == 0 else NX - 1
        at = wbuf.at[mod(x + NX - step, NX), way * 256:way * 256 + 256, wcols(i)]
        return remote(at, at, wfs.at[way, i], wfr.at[way, i], dev(z, y, c, mod(x + step, NX)))

    def wsib(d, i):
        at = wbuf.at[mod(x + d, NX), :, wcols(i)]
        return remote(at, at, wbs.at[d - 1, i], wbr.at[d - 1, i], dev(z, y, 1 - c, x))

    def share(i, way, d):
        at = wbuf.at[mod(x + d, NX), way * 256:way * 256 + 256, wcols(i)]
        return remote(at, at, shs.at[i, way, d - 1], shr.at[i, way, d - 1],
                      dev(mod(z + (1 if way == 0 else NZ - 1), NZ), y, c, x))

    def send_att(d):
        return remote(att_s.at[d - 1], attg.at[x], ats.at[d - 1], atr.at[d - 1], dev(z, y, c, mod(x + d, NX)))

    own_w = pltpu.make_async_copy(w, wbuf.at[x], wls)
    own_w.start()
    bar = pltpu.get_barrier_semaphore()
    peers = [dev(mod(z + r, NZ), y, c, x) for r in (1, NZ - 1)]
    peers += [dev(z, mod(y + d, NY), c, x) for d in range(1, NY)]
    peers += [dev(z, y, c, mod(x + d, NX)) for d in range(1, NX)]
    peers += [dev(z, y, 1 - c, x)]
    for p in peers:
        pl.semaphore_signal(bar, inc=1, device_id=p, device_id_type=pl.DeviceIdType.MESH)
    pl.semaphore_wait(bar, len(peers))

    def need(dest, base_at, origins):
        b = pb[dest]
        g = [gates[e, b] for e in range(TOPK)] + [gates[e, 63 - b] for e in range(TOPK)]
        for i, origin in enumerate(origins):
            late = 63 - pb[origin]
            hit = g[0] == late
            for v in g[1:]:
                hit = hit | (v == late)
            bits[base_at + i] = jnp.where(hit, 1, 0)

    def need1(d, _):
        need(z * 4 + mod(y + d, NY), d * 8, [mod(z + r, NZ) * 4 + y for r in range(NZ)])
        return 0

    def put1(k, r):
        z0 = mod(z + r, NZ)
        if r == 0:
            a, b = kvin[k, 0, 0:HALF], kvin[k, 1, 0:HALF]
        else:
            a, b = col[k][z0, 0], col[k][z0, 1]
        for d in range(1, NY):
            st1[k][r, d - 1] = jnp.where(bits[d * 8 + r] > 0, b, a)
            y1(k, r, d).start()
        if r != 0:
            sel[k][z0 * 4 + y, pl.ds(base, HALF)] = jnp.where(bits[r] > 0, b, a)

    def put_own(k):
        sel[k][me, pl.ds(base, HALF)] = kvin[k, 0]
        sel[k][32, pl.ds(base, HALF)] = kvin[k, 1]
        sib_own(k).start()

    def ring(k, hop):
        for way in range(2):
            if hop:
                z1(k, way, hop).wait_recv()
            if hop < 4:
                z1(k, way, hop + 1).start()

    def rounds(k, hop):
        for r in {0: (0,), 4: (4,)}.get(hop, (NZ - hop, hop)):
            put1(k, r)

    def collect(k, r):
        for d in range(1, NY):
            y1(k, r, d).wait_recv()
        sib(k, r).start()

    drained = set()

    def drain(k, r):
        drained.add((k, r))
        for d in range(1, NY):
            y1(k, r, d).wait_send()

    def sib_in(k):
        for r in range(NZ):
            sib(k, r).wait_recv()
        sib_own(k).wait_recv()

    def find_slots():
        own_early = pb[me]
        ent = [gates[e, own_early] for e in range(TOPK)] + [gates[e, 63 - own_early] for e in range(TOPK)]

        def find(p, at):
            b = pb[p]
            return tuple(jnp.where((g == b) | (g == 63 - b), p, v) for g, v in zip(ent, at))

        at = lax.fori_loop(0, NZ * NY, find, tuple(jnp.int32(0) for _ in ent))
        for i, (g, v) in enumerate(zip(ent, at)):
            slots[i] = jnp.where(g == 63 - own_early, 32, jnp.where(g < 0, me, v))
            valid[i] = jnp.where(g >= 0, 1, 0)

    def unit(u, _):
        di, hp = lax.div(u, jnp.int32(2)), mod(u, 2)
        d = jnp.where(di == 0, 2, jnp.where(di == 1, 1, jnp.where(di == 2, 3, 0)))
        dest = mod(x + d, NX)
        side8 = lax.div(dest, jnp.int32(2)) * 8
        qr = q[pl.ds(pl.multiple_of(dest * 128, 128), 128), pl.ds(pl.multiple_of(hp * 256, 256), 256)]
        qs = jnp.concatenate([qr[:, 0:128], qr[:, 128:256]], axis=0)
        hrow = pl.multiple_of(hp * 256, 256)
        qpos = mod(lax.broadcasted_iota(jnp.int32, (256, 128), 0), 128) + c * HALF + mod(dest, 2) * 128
        lane = lax.broadcasted_iota(jnp.int32, (256, 128), 1)
        m = jnp.full((256, 128), NEG, f32)
        for e in range(TOPK):
            sc = dot_nt(qs, sel_k[slots[side8 + e]])
            best = None
            for t in range(4):
                part = sc[:, t * 128:(t + 1) * 128]
                if e == 0:
                    part = jnp.where(lane + t * 128 <= qpos, part, NEG)
                s_acc[e, t] = part
                best = part if best is None else jnp.maximum(best, part)
            if e:
                best = jnp.where(valid[side8 + e] > 0, best, NEG)
            m = jnp.maximum(m, best)
        m = jnp.max(m, axis=1, keepdims=True)
        total = jnp.zeros((256, 128), f32)
        for e in range(TOPK):
            peak = m if e == 0 else jnp.where(valid[side8 + e] > 0, m, BIG)
            for t in range(4):
                p = jnp.exp2((s_acc[e, t] - peak) * SCALE)
                total = total + p
                p_buf[di, e, pl.ds(hrow, 256), t * 128:(t + 1) * 128] = p.astype(bf16)
        l_buf[di, pl.ds(hrow, 256)] = total
        return 0

    def w_start(i):
        for way in range(2):
            w1(way, i).start()

    def w_forward(i):
        for way in range(2):
            w1(way, i).wait_recv()
            w2(way, i).start()
        wsib(1, i).start()
        wsib(3, i).start()

    def w_last(i):
        for way in range(2):
            w2(way, i).wait_recv()
        wsib(2, i).start()

    def w_share(i):
        for d in range(1, NX):
            for way in range(2):
                share(i, way, d).start()

    def w_shared(i):
        for d in range(1, NX):
            for way in range(2):
                share(i, way, d).wait_recv()
            wsib(d, NW + i).start()

    def w_in():
        for i in range(NW + NS):
            for d in range(1, NX):
                wsib(d, i).wait_recv()

    def values():
        for di, d in enumerate(ORDER):
            dest = mod(x + d, NX)
            side8 = lax.div(dest, jnp.int32(2)) * 8
            acc = jnp.zeros((512, 128), f32)
            for e in range(TOPK):
                acc = acc + jnp.dot(p_buf[di, e], sel_v[slots[side8 + e]], preferred_element_type=f32)
            out = (acc / jnp.sum(l_buf[di], axis=1, keepdims=True)).astype(bf16)
            for h in range(4):
                part = out[h * 128:(h + 1) * 128]
                if d == 0:
                    attg[x, :, h * 128:(h + 1) * 128] = part
                else:
                    att_s[d - 1, :, h * 128:(h + 1) * 128] = part
            if d:
                send_att(d).start()

    acts = {
        "N1": lambda: lax.fori_loop(0, NY, need1, 0), "F": find_slots, "O": put_own, "R": ring, "P": rounds, "C": collect,
        "S": sib_in, "U": lambda a, b: lax.fori_loop(a, b, unit, 0), "W": w_start, "X": w_forward,
        "V": None,
    }
    acts["D"] = drain
    acts["V"] = values
    acts["L"] = w_last
    acts["I"] = w_in
    acts["H"] = w_share
    acts["G"] = w_shared
    for step in STEPS:
        acts[step[0]](*step[1:])
    started = {a[0] for a in STEPS}
    has = {a[:2] for a in STEPS}
    own_w.wait()
    for d in range(1, NX if "V" in started else 0):
        send_att(d).wait_recv()

    def project(n, _):
        cols = pl.ds(pl.multiple_of(n * 512, 512), 512)
        acc = jnp.dot(attg[0], wbuf[0, :, cols], preferred_element_type=f32)
        for i in range(1, NX):
            acc = acc + jnp.dot(attg[i], wbuf[i, :, cols], preferred_element_type=f32)
        o[:, cols] = acc.astype(bf16)
        return 0

    lax.fori_loop(0, 8, project, 0)

    for k in range(2):
        if ("R", k) in has:
            for way in range(2):
                for hop in range(1, 5):
                    z1(k, way, hop).wait_send()
        for r in range(NZ):
            if ("P", k) in has and (k, r) not in drained:
                drain(k, r)
            if ("C", k) in has:
                sib(k, r).wait_send()
        if ("O", k) in has:
            sib_own(k).wait_send()
    if "W" in started:
        for i in range(NW):
            for way in range(2):
                w1(way, i).wait_send()
                w2(way, i).wait_send()
        for i in range(NW + NS):
            for d in range(1, NX):
                wsib(d, i).wait_send()
        for i in range(NS):
            for d in range(1, NX):
                for way in range(2):
                    share(i, way, d).wait_send()
    for d in range(1, NX if "V" in started else 0):
        send_att(d).wait_send()


def body(queries, keyval, gates, pair_block, out_weight):
    kv = keyval.reshape(2, 2, HALF, HD)
    vmem, smem = pl.BlockSpec(memory_space=pltpu.VMEM), pl.BlockSpec(memory_space=pltpu.SMEM)
    dma = pltpu.SemaphoreType.DMA
    scratch = (
        [pltpu.VMEM((33, 512, HD), bf16)] * 2
        + [pltpu.VMEM((NZ, 2, HALF, HD), bf16)] * 2
        + [pltpu.VMEM((NZ, 3, HALF, HD), bf16)] * 2
        + [
            pltpu.VMEM((NX, 512, 4096), bf16),
            pltpu.VMEM((TOPK, 4, 256, 128), f32),
            pltpu.VMEM((NX, TOPK, 512, 512), bf16),
            pltpu.VMEM((NX, 512, 128), f32),
            pltpu.VMEM((3, 128, 512), bf16),
            pltpu.VMEM((NX, 128, 512), bf16),
            pltpu.SMEM((64,), jnp.int32),
            pltpu.SMEM((16,), jnp.int32),
            pltpu.SMEM((16,), jnp.int32),
        ]
        + [dma((2, 2, 4))] * 2
        + [dma((2, NZ, 3))] * 2
        + [dma((2, 9))] * 2
        + [dma((2, NW))] * 4
        + [dma((3, NW + NS))] * 2
        + [dma((NS, 2, 3))] * 2
        + [dma((3,))] * 2
        + [dma]
    )
    return pl.pallas_call(
        kernel,
        out_shape=jax.ShapeDtypeStruct((128, 4096), bf16),
        in_specs=[smem, smem, vmem, vmem, pl.BlockSpec(memory_space=pl.ANY)],
        out_specs=vmem,
        scratch_shapes=scratch,
        name="block_attention",
        cost_estimate=pl.CostEstimate(flops=6 * 2**30, bytes_accessed=8 * 2**20, transcendentals=8 * 2**20),
        compiler_params=pltpu.CompilerParams(
            collective_id=0, has_side_effects=True, vmem_limit_bytes=62 * 2**20),
    )(gates.T, pair_block, queries, kv, out_weight)


def solution(mesh):
    placed = (P("seq", "head"), P(None, "seq", "head"), P(), P(), P("head", None))
    return jax.shard_map(
        body, mesh=mesh, in_specs=placed, out_specs=P(("seq", "head"), None), check_vma=False
    )
```

```python
import jax
import jax.numpy as jnp
from jax import lax
from jax.experimental import pallas as pl
from jax.experimental.pallas import tpu as pltpu
from jax.sharding import PartitionSpec as P

HD = 128
TOPK = 8
HALF = 256
NZ, NY, NX = 8, 4, 4
SCALE = 1.4426950408889634 / 128**0.5
NEG = -1e30
BIG = 1e30
WS = ((0, 384), (384, 384))
WP = 768
WD = ((1536, 512),)
NS, NW = len(WS), len(WS) + len(WD)
ORDER = (2, 1, 3, 0)
STEPS = (
    ("N1",), ("F",), ("B",), ("R", 0, 0), ("W", 0), ("P", 0, 0), ("R", 1, 0), ("O", 0), ("O", 1), ("R", 0, 1),
    ("P", 0, 1), ("R", 1, 1), ("W", 1), ("R", 0, 2), ("P", 0, 2), ("R", 1, 2), ("R", 0, 3), ("P", 0, 3), ("X", 0),
    ("R", 1, 3), ("R", 0, 4), ("P", 0, 4), ("R", 1, 4), ("P", 1, 0), ("C", 0, 0), ("C", 0, 1), ("C", 0, 7),
    ("X", 1), ("L", 0), ("W", 2), ("H", 0), ("P", 1, 1), ("P", 1, 2), ("C", 0, 2), ("C", 0, 6), ("P", 1, 3),
    ("P", 1, 4), ("L", 1), ("H", 1), ("C", 0, 3), ("C", 0, 5), ("C", 0, 4), ("S", 0), ("U", 0, 4), ("C", 1, 0),
    ("C", 1, 1), ("C", 1, 7), ("U", 4, 8), ("X", 2), ("C", 1, 2), ("C", 1, 6), ("C", 1, 3), ("C", 1, 5),
    ("C", 1, 4), ("G", 0), ("S", 1), ("V",), ("G", 1), ("L", 2), ("J", 0), ("J", 1), ("J", 3), ("J", 2),
)
f32, bf16 = jnp.float32, jnp.bfloat16


def mod(a, n):
    return lax.rem(a, jnp.int32(n))


def dot_nt(a, b):
    return lax.dot_general(a, b, (((1,), (1,)), ((), ())), preferred_element_type=f32)


def kernel(gates, pb, q, kvin, w, o, sel_k, sel_v, col_k, col_v, st1_k, st1_v,
           wbuf, s_acc, p_buf, l_buf, att_s, attg, bits, slots, valid,
           z1s, z1r, y1s, y1r, sbs, sbr, wss, wsr, wfs, wfr, wbs, wbr, shs, shr, ats, atr, wls):
    s = lax.axis_index("seq").astype(jnp.int32)
    x = lax.axis_index("head").astype(jnp.int32)
    z = lax.div(s, jnp.int32(8))
    y = mod(lax.div(s, jnp.int32(2)), 4)
    c = mod(s, 2)
    me = z * 4 + y
    sel, col, st1 = (sel_k, sel_v), (col_k, col_v), (st1_k, st1_v)
    base = pl.multiple_of(c * HALF, HALF)

    def dev(zz, yy, cc, xx):
        return ((zz * 4 + yy) * 2 + cc, xx)

    def remote(src, dst, ssem, rsem, device):
        return pltpu.make_async_remote_copy(
            src_ref=src, dst_ref=dst, send_sem=ssem, recv_sem=rsem,
            device_id=device, device_id_type=pl.DeviceIdType.MESH)

    def z1(k, way, hop):
        step = 1 if way == 0 else NZ - 1
        zo = mod(z + (NZ - step) * (hop - 1), NZ)
        lo, n = (0, HALF) if hop < 4 else ((0, HALF // 2) if way == 0 else (HALF // 2, HALF // 2))
        src = kvin.at[k, :, 0:HALF] if hop == 1 else col[k].at[zo, :, lo:lo + n]
        return remote(src, col[k].at[zo, :, lo:lo + n], z1s.at[k, way, hop - 1], z1r.at[k, way, hop - 1],
                      dev(mod(z + step, NZ), y, c, x))

    def y1(k, r, d):
        slot = mod(z + r, NZ) * 4 + y
        return remote(st1[k].at[r, d - 1], sel[k].at[slot, pl.ds(base, HALF)], y1s.at[k, r, d - 1],
                      y1r.at[k, r, d - 1], dev(z, mod(y + d, NY), c, x))

    def sib(k, r):
        at = sel[k].at[pl.ds(mod(z + r, NZ) * 4, 4), pl.ds(base, HALF)]
        return remote(at, at, sbs.at[k, r], sbr.at[k, r], dev(z, y, 1 - c, x))

    def sib_own(k):
        at = sel[k].at[32, pl.ds(base, HALF)]
        return remote(at, at, sbs.at[k, 8], sbr.at[k, 8], dev(z, y, 1 - c, x))

    def wcols(i):
        if NS <= i < NW:
            off, n = WD[i - NS]
        else:
            off, n = WS[i % NW]
            off = off + mod(z + (0 if i < NS else 1), 2) * WP
        return pl.ds(pl.multiple_of(c * 2048 + off, 128), n)

    def w1(way, i):
        step = 1 if way == 0 else NX - 1
        return remote(w.at[:, wcols(i)], wbuf.at[x, :, wcols(i)], wss.at[way, i], wsr.at[way, i],
                      dev(z, y, c, mod(x + step, NX)))

    def w2(way, i):
        step = 1 if way == 0 else NX - 1
        at = wbuf.at[mod(x + NX - step, NX), way * 256:way * 256 + 256, wcols(i)]
        return remote(at, at, wfs.at[way, i], wfr.at[way, i], dev(z, y, c, mod(x + step, NX)))

    def wsib(d, i):
        at = wbuf.at[mod(x + d, NX), :, wcols(i)]
        return remote(at, at, wbs.at[d - 1, i], wbr.at[d - 1, i], dev(z, y, 1 - c, x))

    def share(i, way, d):
        at = wbuf.at[mod(x + d, NX), way * 256:way * 256 + 256, wcols(i)]
        return remote(at, at, shs.at[i, way, d - 1], shr.at[i, way, d - 1],
                      dev(mod(z + (1 if way == 0 else NZ - 1), NZ), y, c, x))

    def send_att(d):
        return remote(att_s.at[d - 1], attg.at[x], ats.at[d - 1], atr.at[d - 1], dev(z, y, c, mod(x + d, NX)))

    own_w = pltpu.make_async_copy(w, wbuf.at[x], wls)
    own_w.start()
    bar = pltpu.get_barrier_semaphore()
    peers = [dev(mod(z + r, NZ), y, c, x) for r in (1, NZ - 1)]
    peers += [dev(z, mod(y + d, NY), c, x) for d in range(1, NY)]
    peers += [dev(z, y, c, mod(x + d, NX)) for d in range(1, NX)]
    peers += [dev(z, y, 1 - c, x)]
    for p in peers:
        pl.semaphore_signal(bar, inc=1, device_id=p, device_id_type=pl.DeviceIdType.MESH)

    def need(dest, base_at, origins):
        b = pb[dest]
        g = [gates[e, b] for e in range(TOPK)] + [gates[e, 63 - b] for e in range(TOPK)]
        for i, origin in enumerate(origins):
            late = 63 - pb[origin]
            hit = g[0] == late
            for v in g[1:]:
                hit = hit | (v == late)
            bits[base_at + i] = jnp.where(hit, 1, 0)

    def need1(d, _):
        need(z * 4 + mod(y + d, NY), d * 8, [mod(z + r, NZ) * 4 + y for r in range(NZ)])
        return 0

    def put1(k, r):
        z0 = mod(z + r, NZ)
        if r == 0:
            a, b = kvin[k, 0, 0:HALF], kvin[k, 1, 0:HALF]
        else:
            a, b = col[k][z0, 0], col[k][z0, 1]
        for d in range(1, NY):
            st1[k][r, d - 1] = jnp.where(bits[d * 8 + r] > 0, b, a)
            y1(k, r, d).start()
        if r != 0:
            sel[k][z0 * 4 + y, pl.ds(base, HALF)] = jnp.where(bits[r] > 0, b, a)

    def put_own(k):
        sel[k][me, pl.ds(base, HALF)] = kvin[k, 0]
        sel[k][32, pl.ds(base, HALF)] = kvin[k, 1]
        sib_own(k).start()

    def ring(k, hop):
        for way in range(2):
            if hop:
                z1(k, way, hop).wait_recv()
            if hop < 4:
                z1(k, way, hop + 1).start()

    def rounds(k, hop):
        for r in {0: (0,), 4: (4,)}.get(hop, (NZ - hop, hop)):
            put1(k, r)

    def collect(k, r):
        for d in range(1, NY):
            y1(k, r, d).wait_recv()
        sib(k, r).start()

    drained = set()

    def drain(k, r):
        drained.add((k, r))
        for d in range(1, NY):
            y1(k, r, d).wait_send()

    def sib_in(k):
        for r in range(NZ):
            sib(k, r).wait_recv()
        sib_own(k).wait_recv()

    def find_slots():
        own_early = pb[me]
        ent = [gates[e, own_early] for e in range(TOPK)] + [gates[e, 63 - own_early] for e in range(TOPK)]

        def find(p, at):
            b = pb[p]
            return tuple(jnp.where((g == b) | (g == 63 - b), p, v) for g, v in zip(ent, at))

        at = lax.fori_loop(0, NZ * NY, find, tuple(jnp.int32(0) for _ in ent))
        for i, (g, v) in enumerate(zip(ent, at)):
            slots[i] = jnp.where(g == 63 - own_early, 32, jnp.where(g < 0, me, v))
            valid[i] = jnp.where(g >= 0, 1, 0)

    def unit(u, _):
        di, hp = lax.div(u, jnp.int32(2)), mod(u, 2)
        d = jnp.where(di == 0, 2, jnp.where(di == 1, 1, jnp.where(di == 2, 3, 0)))
        dest = mod(x + d, NX)
        side8 = lax.div(dest, jnp.int32(2)) * 8
        qr = q[pl.ds(pl.multiple_of(dest * 128, 128), 128), pl.ds(pl.multiple_of(hp * 256, 256), 256)]
        qs = jnp.concatenate([qr[:, 0:128], qr[:, 128:256]], axis=0)
        hrow = pl.multiple_of(hp * 256, 256)
        qpos = mod(lax.broadcasted_iota(jnp.int32, (256, 128), 0), 128) + c * HALF + mod(dest, 2) * 128
        lane = lax.broadcasted_iota(jnp.int32, (256, 128), 1)
        m = jnp.full((256, 128), NEG, f32)
        for e in range(TOPK):
            sc = dot_nt(qs, sel_k[slots[side8 + e]])
            best = None
            for t in range(4):
                part = sc[:, t * 128:(t + 1) * 128]
                if e == 0:
                    part = jnp.where(lane + t * 128 <= qpos, part, NEG)
                s_acc[e, t] = part
                best = part if best is None else jnp.maximum(best, part)
            if e:
                best = jnp.where(valid[side8 + e] > 0, best, NEG)
            m = jnp.maximum(m, best)
        m = jnp.max(m, axis=1, keepdims=True)
        total = jnp.zeros((256, 128), f32)
        for e in range(TOPK):
            peak = m if e == 0 else jnp.where(valid[side8 + e] > 0, m, BIG)
            for t in range(4):
                p = jnp.exp2((s_acc[e, t] - peak) * SCALE)
                total = total + p
                p_buf[di, e, pl.ds(hrow, 256), t * 128:(t + 1) * 128] = p.astype(bf16)
        l_buf[di, pl.ds(hrow, 256)] = total
        return 0

    def w_start(i):
        for way in range(2):
            w1(way, i).start()

    def w_forward(i):
        for way in range(2):
            w1(way, i).wait_recv()
            w2(way, i).start()
        wsib(1, i).start()
        wsib(3, i).start()

    def w_last(i):
        for way in range(2):
            w2(way, i).wait_recv()
        wsib(2, i).start()

    def w_share(i):
        for d in range(1, NX):
            for way in range(2):
                share(i, way, d).start()

    def w_shared(i):
        for d in range(1, NX):
            for way in range(2):
                share(i, way, d).wait_recv()
            wsib(d, NW + i).start()

    def values():
        for di, d in enumerate(ORDER):
            dest = mod(x + d, NX)
            side8 = lax.div(dest, jnp.int32(2)) * 8
            acc = jnp.zeros((512, 128), f32)
            for e in range(TOPK):
                acc = acc + jnp.dot(p_buf[di, e], sel_v[slots[side8 + e]], preferred_element_type=f32)
            out = (acc / jnp.sum(l_buf[di], axis=1, keepdims=True)).astype(bf16)
            for h in range(4):
                part = out[h * 128:(h + 1) * 128]
                if d == 0:
                    attg[x, :, h * 128:(h + 1) * 128] = part
                else:
                    att_s[d - 1, :, h * 128:(h + 1) * 128] = part
            if d:
                send_att(d).start()

    def project(d):
        at = mod(x + d, NX)
        if d:
            send_att(NX - d).wait_recv()
            for i in range(NW + NS):
                wsib(d, i).wait_recv()
        else:
            own_w.wait()
        left = attg[at]
        for n in range(8):
            acc = jnp.dot(left, wbuf[at, :, n * 512:(n + 1) * 512], preferred_element_type=f32)
            for t in range(4):
                part = acc[:, t * 128:(t + 1) * 128]
                if d:
                    part = part + s_acc[n, t, 0:128]
                if d == 2:
                    o[:, n * 512 + t * 128:n * 512 + (t + 1) * 128] = part.astype(bf16)
                else:
                    s_acc[n, t, 0:128] = part

    acts = {
        "N1": lambda: lax.fori_loop(0, NY, need1, 0), "F": find_slots, "O": put_own, "R": ring, "P": rounds, "C": collect,
        "S": sib_in, "U": lambda a, b: lax.fori_loop(a, b, unit, 0), "W": w_start, "X": w_forward,
        "V": None,
    }
    acts["D"] = drain
    acts["J"] = project
    acts["B"] = lambda: pl.semaphore_wait(bar, len(peers))
    acts["V"] = values
    acts["L"] = w_last
    acts["H"] = w_share
    acts["G"] = w_shared
    for step in STEPS:
        acts[step[0]](*step[1:])
    started = {a[0] for a in STEPS}
    has = {a[:2] for a in STEPS}
    for k in range(2):
        if ("R", k) in has:
            for way in range(2):
                for hop in range(1, 5):
                    z1(k, way, hop).wait_send()
        for r in range(NZ):
            if ("P", k) in has and (k, r) not in drained:
                drain(k, r)
            if ("C", k) in has:
                sib(k, r).wait_send()
        if ("O", k) in has:
            sib_own(k).wait_send()
    if "W" in started:
        for i in range(NW):
            for way in range(2):
                w1(way, i).wait_send()
                w2(way, i).wait_send()
        for i in range(NW + NS):
            for d in range(1, NX):
                wsib(d, i).wait_send()
        for i in range(NS):
            for d in range(1, NX):
                for way in range(2):
                    share(i, way, d).wait_send()
    for d in range(1, NX if "V" in started else 0):
        send_att(d).wait_send()


def body(queries, keyval, gates, pair_block, out_weight):
    kv = keyval.reshape(2, 2, HALF, HD)
    vmem, smem = pl.BlockSpec(memory_space=pltpu.VMEM), pl.BlockSpec(memory_space=pltpu.SMEM)
    dma = pltpu.SemaphoreType.DMA
    scratch = (
        [pltpu.VMEM((33, 512, HD), bf16)] * 2
        + [pltpu.VMEM((NZ, 2, HALF, HD), bf16)] * 2
        + [pltpu.VMEM((NZ, 3, HALF, HD), bf16)] * 2
        + [
            pltpu.VMEM((NX, 512, 4096), bf16),
            pltpu.VMEM((TOPK, 4, 256, 128), f32),
            pltpu.VMEM((NX, TOPK, 512, 512), bf16),
            pltpu.VMEM((NX, 512, 128), f32),
            pltpu.VMEM((3, 128, 512), bf16),
            pltpu.VMEM((NX, 128, 512), bf16),
            pltpu.SMEM((64,), jnp.int32),
            pltpu.SMEM((16,), jnp.int32),
            pltpu.SMEM((16,), jnp.int32),
        ]
        + [dma((2, 2, 4))] * 2
        + [dma((2, NZ, 3))] * 2
        + [dma((2, 9))] * 2
        + [dma((2, NW))] * 4
        + [dma((3, NW + NS))] * 2
        + [dma((NS, 2, 3))] * 2
        + [dma((3,))] * 2
        + [dma]
    )
    return pl.pallas_call(
        kernel,
        out_shape=jax.ShapeDtypeStruct((128, 4096), bf16),
        in_specs=[smem, smem, vmem, vmem, pl.BlockSpec(memory_space=pl.ANY)],
        out_specs=vmem,
        scratch_shapes=scratch,
        name="block_attention",
        cost_estimate=pl.CostEstimate(flops=6 * 2**30, bytes_accessed=8 * 2**20, transcendentals=8 * 2**20),
        compiler_params=pltpu.CompilerParams(
            collective_id=0, has_side_effects=True, vmem_limit_bytes=62 * 2**20),
    )(gates.T, pair_block, queries, kv, out_weight)


def solution(mesh):
    placed = (P("seq", "head"), P(None, "seq", "head"), P(), P(), P("head", None))
    return jax.shard_map(
        body, mesh=mesh, in_specs=placed, out_specs=P(("seq", "head"), None), check_vma=False
    )
```
